32 devices in a mesh: tile: 8 (over y, x, core), expo: 4 (over z).
Axes of the slice: x: 2, y: 2, z: 4, core: 2. Of those that a mesh axis runs over, the one named last changes fastest.
Arguments:
- model: bfloat16 [8, 6, 256, 256], P('tile'), may hold values from -6 to 6
- exp_tile: int32 [1536, 1], P(('tile', 'expo')), may hold values from 0 to 7; in each aligned block of 48 rows (0 to 47, 48 to 95, ...) at most 9 rows name the same one
- exp_band: int32 [1536], P(('tile', 'expo')), may hold values from 0 to 5
- exp_offset: int32 [1536, 2], P(('tile', 'expo')), may hold values from 0 to 64
- pixels: bfloat16 [1536, 128, 128], P(('tile', 'expo')), may hold values from -6 to 6
- inv_var: bfloat16 [1536, 128, 128], P(('tile', 'expo')), may hold values from 0.19921875 to 5
- row_op: bfloat16 [6, 128, 192], replicated, may hold values from -0.4375 to 0.4375
- col_op: bfloat16 [6, 128, 192], replicated, may hold values from -0.4375 to 0.4375
Outputs:
- gradient: float32 [8, 6, 256, 256], P('tile', None, 'expo')
The draws below stay inside these ranges and needn't reach their ends.
Inputs may be any that keep to these rules, and one draw needn't show every extreme that they name: `exp_tile`: among the 48 cutouts of one device no tile is named more than 9 times, some tile exactly 9 times; every tile is named by some cutout.
All inputs are finite; a program needn't handle non-finite values.
Results may differ from the reference program's by a relative error of at most 0.0027.
Values may be sent and summed in bfloat16 or wider, within the bound.
A program may use at most 64 MiB of HBM per device.

```python
import math
import jax
import jax.numpy as jnp
import numpy as np
from jax import lax

BANDS = 6
P_SIZE = 256
Q = 192
M = 128
E_DEV = 48
TILES = 8
EXPOS = 1536
CAP = 9


def set_ends(result, stream_key, low, largest):
    longest = result.shape.index(max(result.shape))
    spots = []
    for shift in (0, 1):
        where = [jax.random.randint(jax.random.fold_in(stream_key, axis), (), 0, length) for axis, length in enumerate(result.shape)]
        where[longest] = (where[longest] + shift) % result.shape[longest]
        spots.append(tuple(where))
    return result.at[spots[0]].set(low).at[spots[1]].set(largest)


def shard_levels(rng, shape, split, least, top_value):
    def one(axis_at, shards_of):
        steps = jax.random.uniform(jax.random.fold_in(jax.random.fold_in(rng, 6), axis_at), (shards_of,), jnp.float32, least / len(split), top_value / len(split))
        return jnp.repeat(jnp.exp(steps), shape[axis_at] // shards_of).reshape((-1,) + (1,) * (len(shape) - axis_at - 1))

    level = one(*split[0])
    for cut in split[1:]:
        level = level * one(*cut)
    return level


def shared_out(rng, own, number, rows, number_of, top, most, skew):
    order = jax.random.permutation(rng, number_of)
    packed, common = load_shares(number_of, rows * top, most, skew, True), load_shares(number_of, rows * top, most, skew, False)
    places = jnp.arange(number_of)

    def named(lengths, offset_by):
        used = int((lengths > 0).sum())
        fixed = max(1, used // 4)
        passed = fixed + (places - fixed + offset_by * (used - fixed)) % max(1, number_of - fixed)
        return jnp.zeros((number_of,), jnp.int32).at[order[jnp.where(places < fixed, places, passed)]].set(jnp.asarray(lengths, jnp.int32))

    lengths = jnp.where(number % 4 == 0, named(packed, number // 4), named(common, number - number // 4 - 1))
    mixed = jax.random.permutation(jax.random.fold_in(own, 3), number_of)
    source_of, taker = mixed[0:number_of // 2 * 2:2], mixed[1:number_of // 2 * 2:2]
    room = jnp.minimum(lengths[source_of] - 1, most - lengths[taker]) // 2
    room = jnp.where((source_of == order[0]) | (taker == order[0]) | (lengths[taker] == 0), 0, jnp.maximum(room, 0))
    passed = jax.random.randint(jax.random.fold_in(own, 4), (number_of // 2,), 0, 1 << 20) % (room + 1)
    lengths = lengths.at[source_of].add(-passed).at[taker].add(passed)
    members = jnp.searchsorted(jnp.cumsum(lengths), jnp.arange(rows * top), side="right").astype(jnp.int32)
    listing = members.reshape(top, rows).T
    listing = listing[jax.random.permutation(jax.random.fold_in(own, 1), rows)]
    offset_by = jax.random.randint(jax.random.fold_in(own, 2), (rows, 1), 0, top)
    return jnp.take_along_axis(listing, (jnp.arange(top)[None, :] + offset_by) % top, axis=1)


def load_shares(count, total, limit, skew, full):
    loads = [(1 << 20) // math.isqrt(standing ** skew) + 1 for standing in range(1, count + 1)]
    largest = limit if full else min(limit, max(-(-total // count), total * loads[0] // sum(loads)))
    least = 1 if total - largest >= count - 1 else 0
    holding, surplus = [largest] + [least] * (count - 1), total - largest - least * (count - 1)
    while surplus > 0:
        free = [i for i in range(1, count) if holding[i] < largest] or [i for i in range(1, count) if holding[i] < limit]
        mass, budget = sum([loads[i] for i in free]), surplus
        for i in free:
            extra = min(limit - holding[i], max(1, budget * loads[i] // mass), surplus)
            holding[i] = holding[i] + extra
            surplus = surplus - extra
    return np.array(holding)


def scatter_about(own_key, extent, width, bound, pieces=(), held_as=jnp.bfloat16):
    loudness = shard_levels(own_key, extent, pieces, -0.22, 0.18) if pieces else 1.0
    values = jax.random.normal(own_key, extent, jnp.float32) * width * loudness
    return jnp.minimum(jnp.maximum(values, -bound), bound).astype(held_as)


def setup_inputs(seed: int = 0) -> dict:
    keys = jax.random.split(jax.random.key(seed), 9)
    model = scatter_about(keys[0], (TILES, BANDS, P_SIZE, P_SIZE), 1.0, 6.0, ((0, 8),))
    exp_tile_keys = jax.random.split(jax.random.fold_in(keys[1], 1), EXPOS // E_DEV)
    exp_tile_turns = jax.random.permutation(jax.random.fold_in(keys[1], 3), EXPOS // E_DEV)
    exp_tile = jax.vmap(lambda own, number: shared_out(jax.random.fold_in(keys[1], 2), own, number, E_DEV, TILES, 1, CAP, 2))(exp_tile_keys, exp_tile_turns).reshape((EXPOS, 1))
    exp_band = set_ends(jax.random.randint(keys[2], (EXPOS,), 0, BANDS), jax.random.fold_in(keys[2], 1), 0, BANDS - 1).astype(jnp.int32)
    exp_offset = set_ends(jax.random.randint(keys[3], (EXPOS, 2), 0, P_SIZE - Q + 1), jax.random.fold_in(keys[3], 1), 0, P_SIZE - Q).astype(jnp.int32)
    pixels = scatter_about(keys[4], (EXPOS, M, M), 1.0, 6.0, ((0, 32),))
    inv_var = jnp.clip(jnp.exp(math.log(5.0) - 3.2227897 * jax.random.uniform(keys[5], (EXPOS, M, M), jnp.float32) ** shard_levels(keys[5], (EXPOS, M, M), ((0, 32),), -0.2, 0.2)), 0.19921875, 5.0).astype(jnp.bfloat16)
    row_op = scatter_about(keys[6], (BANDS, M, Q), Q ** -0.5, 0.4375)
    col_op = scatter_about(keys[7], (BANDS, M, Q), Q ** -0.5, 0.4375)
    return dict(model=model, exp_tile=exp_tile, exp_band=exp_band, exp_offset=exp_offset, pixels=pixels, inv_var=inv_var, row_op=row_op, col_op=col_op)


def adjoint_block(windows, bands, pixels, inv_var, row_op, col_op):
    rows = row_op[bands].astype(jnp.float32)
    cols = col_op[bands].astype(jnp.float32)
    half = jnp.einsum("nmq,nqk->nmk", rows, windows.astype(jnp.float32)).astype(jnp.bfloat16)
    predicted = jnp.einsum("nmk,nlk->nml", half.astype(jnp.float32), cols)
    weighted = (inv_var.astype(jnp.float32) * (predicted - pixels.astype(jnp.float32))).astype(jnp.bfloat16)
    back = jnp.einsum("nmq,nml->nql", rows, weighted.astype(jnp.float32)).astype(jnp.bfloat16)
    return jnp.einsum("nql,nlk->nqk", back.astype(jnp.float32), cols).astype(jnp.bfloat16)


def reference(model, exp_tile, exp_band, exp_offset, pixels, inv_var, row_op, col_op):
    tiles = exp_tile[:, 0].astype(jnp.int32)
    bands = exp_band.astype(jnp.int32)
    offsets = exp_offset.astype(jnp.int32)

    def take(tile_id, band_id, corner):
        return lax.dynamic_slice(model, (tile_id, band_id, corner[0], corner[1]), (1, 1, Q, Q))[0, 0]

    blocks = EXPOS // E_DEV

    def per_block(items):
        tile_b, band_b, corner_b, pix_b, ivar_b = items
        windows = jax.vmap(take)(tile_b, band_b, corner_b)
        return adjoint_block(windows, band_b, pix_b, ivar_b, row_op, col_op)

    adjoint = lax.map(per_block, (tiles.reshape(blocks, E_DEV), bands.reshape(blocks, E_DEV),
                                  offsets.reshape(blocks, E_DEV, 2), pixels.reshape(blocks, E_DEV, M, M),
                                  inv_var.reshape(blocks, E_DEV, M, M)))
    adjoint = adjoint.reshape(EXPOS, Q, Q)

    def place(index, total):
        start = (tiles[index], bands[index], offsets[index, 0], offsets[index, 1])
        window = lax.dynamic_slice(total, start, (1, 1, Q, Q))
        added = window + adjoint[index].astype(jnp.float32)[None, None]
        return lax.dynamic_update_slice(total, added, start)

    gradient = jnp.zeros((TILES, BANDS, P_SIZE, P_SIZE), jnp.float32)
    return lax.fori_loop(0, EXPOS, place, gradient)
```

```python
import functools

import jax
import jax.numpy as jnp
from jax import lax
from jax.experimental import pallas as pl
from jax.experimental.pallas import tpu as pltpu
from jax.sharding import PartitionSpec as P


def slot_layout(exp_tile, exp_band, exp_offset, owners, capacity):
    target = exp_tile[:, 0]
    count = target.shape[0]
    order = jnp.arange(count, dtype=jnp.int32)
    before = (target[:, None] == target[None, :]) & (order[None, :] < order[:, None])
    rank = jnp.sum(before.astype(jnp.int32), axis=1)
    slot = target * capacity + rank
    fields = jnp.stack(
        [jnp.ones_like(target), exp_band, exp_offset[:, 0], exp_offset[:, 1], order], axis=1
    )
    slot_ids = jnp.arange(owners * capacity, dtype=jnp.int32)
    slot_hot = (slot[:, None] == slot_ids[None, :]).astype(jnp.int32)
    return jnp.sum(slot_hot[:, :, None] * fields[:, None, :], axis=0)


def compute_kernel(capacity, meta, data, model, row_wide, col_wide, row_tall, acc):
    group = pl.program_id(0)
    side = acc.shape[-1]
    reach = row_tall.shape[1] - side

    @pl.when(group == 0)
    def _():
        acc[...] = jnp.zeros_like(acc)

    def one_slot(s, carry):
        at = group * capacity + s

        @pl.when(meta[0, at] > 0)
        def _():
            band, row, col = meta[1, at], meta[2, at], meta[3, at]
            r = pltpu.roll(row_wide[band], row, 1).astype(jnp.bfloat16)
            c = pltpu.roll(col_wide[band], col, 1).astype(jnp.bfloat16)
            rt = row_tall[band, pl.ds(reach - row, side), :].astype(jnp.bfloat16)
            half = jnp.dot(r, model[band], preferred_element_type=jnp.float32).astype(jnp.bfloat16)
            predicted = lax.dot_general(
                half, c, (((1,), (1,)), ((), ())), preferred_element_type=jnp.float32
            )
            pixels = data[0, s, 0].astype(jnp.float32)
            inv_var = data[0, s, 1].astype(jnp.float32)
            weighted = (inv_var * (predicted - pixels)).astype(jnp.bfloat16)
            back = jnp.dot(rt, weighted, preferred_element_type=jnp.float32).astype(jnp.bfloat16)
            adjoint = jnp.dot(back, c, preferred_element_type=jnp.float32).astype(jnp.bfloat16)
            acc[band] += adjoint.astype(jnp.float32)

        return carry

    lax.fori_loop(0, capacity, one_slot, 0)


def local(model, exp_tile, exp_band, exp_offset, pixels, inv_var, row_op, col_op):
    owners = lax.axis_size("tile")
    count, m, _ = pixels.shape
    capacity = max(2, 3 * count // (2 * owners))
    bands, side = model.shape[1], model.shape[2]
    q = row_op.shape[2]
    reach = side - q
    requests = slot_layout(exp_tile, exp_band, exp_offset, owners, capacity)
    picked = requests[:, 4]
    outgoing = jnp.stack([pixels[picked], inv_var[picked]], axis=1)
    received = lax.all_to_all(requests, "tile", split_axis=0, concat_axis=0, tiled=True)
    arrived = lax.all_to_all(outgoing, "tile", split_axis=0, concat_axis=0, tiled=True)
    arrived = arrived.reshape(owners, capacity, 2, m, m)
    row_wide = jnp.pad(row_op.astype(jnp.float32), ((0, 0), (0, 0), (0, reach)))
    col_wide = jnp.pad(col_op.astype(jnp.float32), ((0, 0), (0, 0), (0, reach)))
    row_tall = jnp.pad(
        jnp.swapaxes(row_op.astype(jnp.float32), 1, 2), ((0, 0), (reach, reach), (0, 0))
    )
    full = lambda x: pl.BlockSpec(x.shape, lambda g, meta: (0,) * x.ndim)
    partial = pl.pallas_call(
        functools.partial(compute_kernel, capacity),
        grid_spec=pltpu.PrefetchScalarGridSpec(
            num_scalar_prefetch=1,
            grid=(owners,),
            in_specs=[
                pl.BlockSpec((1, capacity, 2, m, m), lambda g, meta: (g, 0, 0, 0, 0)),
                full(model[0]),
                full(row_wide),
                full(col_wide),
                full(row_tall),
            ],
            out_specs=pl.BlockSpec((bands, side, side), lambda g, meta: (0, 0, 0)),
        ),
        out_shape=jax.ShapeDtypeStruct((bands, side, side), jnp.float32),
        compiler_params=pltpu.CompilerParams(vmem_limit_bytes=48 * 1024 * 1024),
    )(received.T, arrived, model[0], row_wide, col_wide, row_tall)
    return lax.psum_scatter(partial[None], "expo", scatter_dimension=2, tiled=True)


def solution(mesh):
    in_specs = (
        P("tile", None, None, None),
        P(("tile", "expo"), None),
        P(("tile", "expo")),
        P(("tile", "expo"), None),
        P(("tile", "expo"), None, None),
        P(("tile", "expo"), None, None),
        P(),
        P(),
    )
    out_specs = P("tile", None, "expo", None)
    return jax.shard_map(local, mesh=mesh, in_specs=in_specs, out_specs=out_specs, check_vma=False)
```

```python
import functools

import jax
import jax.numpy as jnp
from jax import lax
from jax.experimental import pallas as pl
from jax.experimental.pallas import tpu as pltpu
from jax.sharding import PartitionSpec as P

AHEAD = 4
LANES = 128
FIELDS = 8


def slot_layout(exp_tile, exp_band, exp_offset, owners):
    target = exp_tile[:, 0]
    count = target.shape[0]
    order = jnp.arange(count, dtype=jnp.int32)
    before = (target[:, None] == target[None, :]) & (order[None, :] < order[:, None])
    rank = jnp.sum(before.astype(jnp.int32), axis=1)
    zero = jnp.zeros_like(target)
    fields = jnp.stack(
        [zero + 1, exp_band, exp_offset[:, 0], exp_offset[:, 1], order, zero, zero, zero], axis=1
    )
    owner_hot = target[:, None] == jnp.arange(owners, dtype=jnp.int32)[None, :]
    slot_hot = rank[:, None] == jnp.arange(LANES, dtype=jnp.int32)[None, :]
    hot = owner_hot[:, :, None, None] & slot_hot[:, None, None, :]
    return jnp.sum(jnp.where(hot, fields[:, None, :, None], 0), axis=0)


def partner(me, step, owners):
    if owners == 8:
        third = (step + 1) // 4 - step // 4 - (step + 1) // 8 + step // 8
        fourth = step // 4 - (step + 3) // 8
        step = step + third - fourth
    out = 0
    bit = 1
    while bit < owners:
        out = out + bit * (((me // bit) % 2 + (step // bit) % 2) % 2)
        bit *= 2
    return out


def kernel(
    owners, groups, capacity,
    meta_smem, meta_out, pixels, inv_var, model, row_op, col_op,
    out,
    send, recv, meta_in, meta_s, row_wide, col_wide, row_tall, backs, cols, acc, zsend, zrecv,
    send_sem, recv_sem, msend_sem, mrecv_sem, local_sem, zsend_sem, zrecv_sem,
):
    me = lax.axis_index("tile")
    depth = lax.axis_index("expo")
    bands, side, _ = acc.shape
    m, q = row_op.shape[1:]
    reach = side - q
    rows = side // groups
    together = 3 if capacity % 3 == 0 else (2 if capacity % 2 == 0 else 1)

    barrier = pltpu.get_barrier_semaphore()

    def greet_tile(j, carry):
        pl.semaphore_signal(
            barrier, inc=1, device_id={"tile": partner(me, j, owners)},
            device_id_type=pl.DeviceIdType.MESH,
        )
        return carry

    def greet_expo(j, carry):
        pl.semaphore_signal(
            barrier, inc=1, device_id={"expo": lax.rem(depth + j, groups)},
            device_id_type=pl.DeviceIdType.MESH,
        )
        return carry

    lax.fori_loop(1, owners, greet_tile, 0)
    lax.fori_loop(1, groups, greet_expo, 0)

    def fill(j, into):
        peer = partner(me, j, owners)

        def one(s, carry):
            e = meta_smem[peer, 4, s]
            into[j, s, 0] = pixels[e]
            into[j, s, 1] = inv_var[e]
            return carry

        lax.fori_loop(0, capacity, one, 0)

    def data_copy(j):
        return pltpu.make_async_remote_copy(
            send.at[j], recv.at[j], send_sem.at[j], recv_sem.at[j],
            device_id={"tile": partner(me, j, owners)}, device_id_type=pl.DeviceIdType.MESH,
        )

    def meta_copy(j):
        peer = partner(me, j, owners)
        return pltpu.make_async_remote_copy(
            meta_out.at[peer], meta_in.at[j], msend_sem.at[j], mrecv_sem.at[j],
            device_id={"tile": peer}, device_id_type=pl.DeviceIdType.MESH,
        )

    fill(1, send)
    pl.semaphore_wait(barrier, owners + groups - 2)

    def push(j, carry):
        meta_copy(j).start()

        @pl.when(j > 1)
        def _():
            fill(j, send)

        data_copy(j).start()
        return carry

    ahead = min(AHEAD, owners - 1)
    lax.fori_loop(1, ahead + 1, push, 0)

    fill(0, recv)
    acc[...] = jnp.zeros_like(acc)
    cols[capacity] = jnp.zeros_like(cols[capacity])

    def widen(b, carry):
        zeros = jnp.zeros((m, reach), jnp.float32)
        r = jnp.concatenate([row_op[b].astype(jnp.float32), zeros], axis=1)
        row_wide[b] = r
        col_wide[b] = jnp.concatenate([col_op[b].astype(jnp.float32), zeros], axis=1)
        row_tall[b, 0:reach, :] = jnp.zeros((reach, m), jnp.float32)
        row_tall[b, reach : reach + side, :] = r.T
        return carry

    lax.fori_loop(0, bands, widen, 0)

    def compute(j):
        def some_slots(t, carry):
            slots = [t * together + u for u in range(together)]
            wide, cut = [], []
            for s in slots:
                band, row, col = meta_s[1, s], meta_s[2, s], meta_s[3, s]
                r = pltpu.roll(row_wide[band], row, 1).astype(jnp.bfloat16)
                c = pltpu.roll(col_wide[band], col, 1).astype(jnp.bfloat16)
                rt = row_tall[band, pl.ds(reach - row, side), :].astype(jnp.bfloat16)
                cols[s] = c
                wide.append((r, c, rt, band))
            halfs = [
                jnp.dot(r, model[band], preferred_element_type=jnp.float32).astype(jnp.bfloat16)
                for r, c, rt, band in wide
            ]
            predicted = [
                lax.dot_general(
                    h, w[1], (((1,), (1,)), ((), ())), preferred_element_type=jnp.float32
                )
                for h, w in zip(halfs, wide)
            ]
            weighted = [
                (
                    recv[j, s, 1].astype(jnp.float32) * (p - recv[j, s, 0].astype(jnp.float32))
                ).astype(jnp.bfloat16)
                for p, s in zip(predicted, slots)
            ]
            for w, x, s in zip(wide, weighted, slots):
                backs[s] = jnp.dot(w[2], x, preferred_element_type=jnp.float32).astype(
                    jnp.bfloat16
                )
            return carry

        lax.fori_loop(0, capacity // together, some_slots, 0)

        def one_band(b, carry):
            left = jnp.concatenate([backs[s] for s in range(capacity)], axis=1)
            right = []
            for s in range(capacity):
                mine = (meta_s[0, s] > 0) & (meta_s[1, s] == b)
                right.append(cols[jnp.where(mine, s, capacity)])
            acc[b] += jnp.dot(
                left, jnp.concatenate(right, axis=0), preferred_element_type=jnp.float32
            )
            return carry

        lax.fori_loop(0, bands, one_band, 0)

    def fetch_meta(source):
        copy = pltpu.make_async_copy(source, meta_s, local_sem)
        copy.start()
        copy.wait()

    fetch_meta(meta_out.at[me])
    compute(0)

    def turn(j, carry):
        meta_copy(j).wait_recv()
        data_copy(j).wait_recv()

        @pl.when(j + ahead < owners)
        def _():
            push(j + ahead, 0)

        fetch_meta(meta_in.at[j])
        compute(j)
        return carry

    lax.fori_loop(1, owners, turn, 0)

    def block(z):
        return pl.ds(pl.multiple_of(z * rows, rows), rows)

    def z_copy(j):
        return pltpu.make_async_remote_copy(
            zsend.at[j], zrecv.at[j], zsend_sem.at[j], zrecv_sem.at[j],
            device_id={"expo": lax.rem(depth + j, groups)}, device_id_type=pl.DeviceIdType.MESH,
        )

    def z_push(j, carry):
        zsend[j] = acc[:, block(lax.rem(depth + j, groups)), :].astype(jnp.bfloat16)
        z_copy(j).start()
        return carry

    lax.fori_loop(1, groups, z_push, 0)
    out[...] = acc[:, block(depth), :]

    def z_sum(j, carry):
        z_copy(j).wait_recv()
        out[...] += zrecv[j].astype(jnp.float32)
        return carry

    lax.fori_loop(1, groups, z_sum, 0)

    def finish(j, carry):
        meta_copy(j).wait_send()
        data_copy(j).wait_send()
        return carry

    lax.fori_loop(1, owners, finish, 0)

    def z_finish(j, carry):
        z_copy(j).wait_send()
        return carry

    lax.fori_loop(1, groups, z_finish, 0)


def local(model, exp_tile, exp_band, exp_offset, pixels, inv_var, row_op, col_op):
    owners = lax.axis_size("tile")
    groups = lax.axis_size("expo")
    count, m, _ = pixels.shape
    capacity = max(2, 3 * count // (2 * owners))
    bands, side = model.shape[1], model.shape[2]
    q = row_op.shape[2]
    reach = side - q
    rows = side // groups
    requests = slot_layout(exp_tile, exp_band, exp_offset, owners)
    vmem = pl.BlockSpec(memory_space=pltpu.VMEM)
    dma = pltpu.SemaphoreType.DMA
    result = pl.pallas_call(
        functools.partial(kernel, owners, groups, capacity),
        out_shape=jax.ShapeDtypeStruct((bands, rows, side), jnp.float32),
        in_specs=[pl.BlockSpec(memory_space=pltpu.SMEM)] + [vmem] * 6,
        out_specs=vmem,
        scratch_shapes=[
            pltpu.VMEM((owners, capacity, 2, m, m), jnp.bfloat16),
            pltpu.VMEM((owners, capacity, 2, m, m), jnp.bfloat16),
            pltpu.VMEM((owners, FIELDS, LANES), jnp.int32),
            pltpu.SMEM((FIELDS, LANES), jnp.int32),
            pltpu.VMEM((bands, m, side), jnp.float32),
            pltpu.VMEM((bands, m, side), jnp.float32),
            pltpu.VMEM((bands, reach + side, m), jnp.float32),
            pltpu.VMEM((capacity, side, m), jnp.bfloat16),
            pltpu.VMEM((capacity + 1, m, side), jnp.bfloat16),
            pltpu.VMEM((bands, side, side), jnp.float32),
            pltpu.VMEM((groups, bands, rows, side), jnp.bfloat16),
            pltpu.VMEM((groups, bands, rows, side), jnp.bfloat16),
            dma((owners,)),
            dma((owners,)),
            dma((owners,)),
            dma((owners,)),
            dma,
            dma((groups,)),
            dma((groups,)),
        ],
        compiler_params=pltpu.CompilerParams(
            collective_id=0, has_side_effects=True, vmem_limit_bytes=56 * 1024 * 1024
        ),
    )(requests, requests, pixels, inv_var, model[0], row_op, col_op)
    return result[None]


def solution(mesh):
    in_specs = (
        P("tile", None, None, None),
        P(("tile", "expo"), None),
        P(("tile", "expo")),
        P(("tile", "expo"), None),
        P(("tile", "expo"), None, None),
        P(("tile", "expo"), None, None),
        P(),
        P(),
    )
    out_specs = P("tile", None, "expo", None)
    return jax.shard_map(local, mesh=mesh, in_specs=in_specs, out_specs=out_specs, check_vma=False)
```

```python
import functools

import jax
import jax.numpy as jnp
from jax import lax
from jax.experimental import pallas as pl
from jax.experimental.pallas import tpu as pltpu
from jax.sharding import PartitionSpec as P

AHEAD = 5
LANES = 128


def slot_layout(exp_tile, exp_band, exp_offset, owners):
    target = exp_tile[:, 0]
    count = target.shape[0]
    order = jnp.arange(count, dtype=jnp.int32)
    before = (target[:, None] == target[None, :]) & (order[None, :] < order[:, None])
    rank = jnp.sum(before.astype(jnp.int32), axis=1)
    packed = 1 + 2 * exp_band + 16 * exp_offset[:, 0] + 2048 * exp_offset[:, 1] + 262144 * order
    owner_hot = target[:, None] == jnp.arange(owners, dtype=jnp.int32)[None, :]
    slot_hot = rank[:, None] == jnp.arange(LANES, dtype=jnp.int32)[None, :]
    hot = owner_hot[:, :, None] & slot_hot[:, None, :]
    return jnp.sum(jnp.where(hot, packed[:, None, None], 0), axis=0)


def partner(me, step, owners):
    if owners == 8:
        third = (step + 1) // 4 - step // 4 - (step + 1) // 8 + step // 8
        fourth = step // 4 - (step + 3) // 8
        step = step + third - fourth
    out = 0
    bit = 1
    while bit < owners:
        out = out + bit * (((me // bit) % 2 + (step // bit) % 2) % 2)
        bit *= 2
    return out


def kernel(
    owners, groups, capacity,
    meta_smem, meta_out, pixels_hbm, inv_var_hbm, model_hbm, row_hbm, col_hbm,
    out,
    pixels, inv_var, model, row_op, col_op, load_sem,
    send, recv, meta_in, meta_s, row_wide, col_wide, row_tall, backs, cols, acc, zsend, zrecv,
    send_sem, recv_sem, msend_sem, mrecv_sem, local_sem, zsend_sem, zrecv_sem,
):
    me = lax.axis_index("tile")
    depth = lax.axis_index("expo")
    bands, side, _ = acc.shape
    q, m = row_op.shape[1:]
    reach = side - q
    rows = side // groups
    together = 3 if capacity % 3 == 0 else (2 if capacity % 2 == 0 else 1)

    loads = [
        pltpu.make_async_copy(source, target, load_sem.at[i])
        for i, (source, target) in enumerate(
            (
                (pixels_hbm, pixels),
                (inv_var_hbm, inv_var),
                (row_hbm, row_op),
                (col_hbm, col_op),
                (model_hbm, model),
            )
        )
    ]
    for load in loads:
        load.start()
    barrier = pltpu.get_barrier_semaphore()

    def greet_tile(j, carry):
        pl.semaphore_signal(
            barrier, inc=1, device_id={"tile": partner(me, j, owners)},
            device_id_type=pl.DeviceIdType.MESH,
        )
        return carry

    def greet_expo(j, carry):
        pl.semaphore_signal(
            barrier, inc=1, device_id={"expo": lax.rem(depth + j, groups)},
            device_id_type=pl.DeviceIdType.MESH,
        )
        return carry

    lax.fori_loop(1, owners, greet_tile, 0)
    lax.fori_loop(1, groups, greet_expo, 0)

    def fill(j, into):
        peer = partner(me, j, owners)

        def one(s, carry):
            e = meta_smem[peer, s] // 262144
            into[j, s, 0] = pixels[e]
            into[j, s, 1] = inv_var[e]
            return carry

        lax.fori_loop(0, capacity, one, 0)

    def data_copy(j):
        return pltpu.make_async_remote_copy(
            send.at[j], recv.at[j], send_sem.at[j], recv_sem.at[j],
            device_id={"tile": partner(me, j, owners)}, device_id_type=pl.DeviceIdType.MESH,
        )

    def meta_copy(j):
        peer = partner(me, j, owners)
        return pltpu.make_async_remote_copy(
            meta_out.at[peer], meta_in.at[j], msend_sem.at[j], mrecv_sem.at[j],
            device_id={"tile": peer}, device_id_type=pl.DeviceIdType.MESH,
        )

    loads[0].wait()
    loads[1].wait()
    fill(1, send)
    pl.semaphore_wait(barrier, owners + groups - 2)

    def push(j, carry):
        meta_copy(j).start()

        @pl.when(j > 1)
        def _():
            fill(j, send)

        data_copy(j).start()
        return carry

    ahead = min(AHEAD, owners - 1)
    lax.fori_loop(1, ahead + 1, push, 0)

    fill(0, recv)
    acc[...] = jnp.zeros_like(acc)
    cols[capacity] = jnp.zeros_like(cols[capacity])

    for load in loads[2:]:
        load.wait()

    def widen(b, carry):
        zeros = jnp.zeros((reach, m), jnp.float32)
        r = jnp.concatenate([row_op[b].astype(jnp.float32), zeros], axis=0)
        c = jnp.concatenate([col_op[b].astype(jnp.float32), zeros], axis=0)
        row_wide[b] = r.T
        col_wide[b] = c.T
        row_tall[b, 0:reach, :] = zeros
        row_tall[b, reach : reach + side, :] = r
        return carry

    lax.fori_loop(0, bands, widen, 0)

    def compute(j):
        def some_slots(t, carry):
            slots = [t * together + u for u in range(together)]
            wide, cut = [], []
            for s in slots:
                code = meta_s[0, s]
                band, row, col = code // 2 % 8, code // 16 % 128, code // 2048 % 128
                r = pltpu.roll(row_wide[band], row, 1).astype(jnp.bfloat16)
                c = pltpu.roll(col_wide[band], col, 1).astype(jnp.bfloat16)
                rt = row_tall[band, pl.ds(reach - row, side), :].astype(jnp.bfloat16)
                cols[s] = c
                wide.append((r, c, rt, band))
            halfs = [
                jnp.dot(r, model[band], preferred_element_type=jnp.float32).astype(jnp.bfloat16)
                for r, c, rt, band in wide
            ]
            predicted = [
                lax.dot_general(
                    h, w[1], (((1,), (1,)), ((), ())), preferred_element_type=jnp.float32
                )
                for h, w in zip(halfs, wide)
            ]
            weighted = [
                (
                    recv[j, s, 1].astype(jnp.float32) * (p - recv[j, s, 0].astype(jnp.float32))
                ).astype(jnp.bfloat16)
                for p, s in zip(predicted, slots)
            ]
            for w, x, s in zip(wide, weighted, slots):
                backs[s] = jnp.dot(w[2], x, preferred_element_type=jnp.float32).astype(
                    jnp.bfloat16
                )
            return carry

        lax.fori_loop(0, capacity // together, some_slots, 0)

        def one_band(b, carry):
            left = jnp.concatenate([backs[s] for s in range(capacity)], axis=1)
            right = []
            for s in range(capacity):
                mine = meta_s[0, s] % 16 == 2 * b + 1
                right.append(cols[jnp.where(mine, s, capacity)])
            acc[b] += jnp.dot(
                left, jnp.concatenate(right, axis=0), preferred_element_type=jnp.float32
            )
            return carry

        lax.fori_loop(0, bands, one_band, 0)

    def fetch_meta(source):
        copy = pltpu.make_async_copy(source, meta_s, local_sem)
        copy.start()
        copy.wait()

    fetch_meta(meta_out.at[me])
    compute(0)

    def turn(j, carry):
        meta_copy(j).wait_recv()
        data_copy(j).wait_recv()

        @pl.when(j + ahead < owners)
        def _():
            push(j + ahead, 0)

        fetch_meta(meta_in.at[j])
        compute(j)
        return carry

    lax.fori_loop(1, owners, turn, 0)

    def block(z):
        return pl.ds(pl.multiple_of(z * rows, rows), rows)

    def z_copy(j):
        return pltpu.make_async_remote_copy(
            zsend.at[j], zrecv.at[j], zsend_sem.at[j], zrecv_sem.at[j],
            device_id={"expo": lax.rem(depth + j, groups)}, device_id_type=pl.DeviceIdType.MESH,
        )

    def z_push(j, carry):
        zsend[j] = acc[:, block(lax.rem(depth + j, groups)), :].astype(jnp.bfloat16)
        z_copy(j).start()
        return carry

    lax.fori_loop(1, groups, z_push, 0)
    out[...] = acc[:, block(depth), :]

    def z_sum(j, carry):
        z_copy(j).wait_recv()
        out[...] += zrecv[j].astype(jnp.float32)
        return carry

    lax.fori_loop(1, groups, z_sum, 0)

    def finish(j, carry):
        meta_copy(j).wait_send()
        data_copy(j).wait_send()
        return carry

    lax.fori_loop(1, owners, finish, 0)

    def z_finish(j, carry):
        z_copy(j).wait_send()
        return carry

    lax.fori_loop(1, groups, z_finish, 0)


def local(model, exp_tile, exp_band, exp_offset, pixels, inv_var, row_op, col_op):
    owners = lax.axis_size("tile")
    groups = lax.axis_size("expo")
    count, m, _ = pixels.shape
    capacity = max(2, 3 * count // (2 * owners))
    bands, side = model.shape[1], model.shape[2]
    q = row_op.shape[2]
    reach = side - q
    rows = side // groups
    packed = slot_layout(exp_tile, exp_band, exp_offset, owners)
    row_tr, col_tr = jnp.swapaxes(row_op, 1, 2), jnp.swapaxes(col_op, 1, 2)
    hbm = pl.BlockSpec(memory_space=pl.ANY)
    vmem = pl.BlockSpec(memory_space=pltpu.VMEM)
    dma = pltpu.SemaphoreType.DMA
    result = pl.pallas_call(
        functools.partial(kernel, owners, groups, capacity),
        out_shape=jax.ShapeDtypeStruct((bands, rows, side), jnp.float32),
        in_specs=[pl.BlockSpec(memory_space=pltpu.SMEM), vmem] + [hbm] * 5,
        out_specs=vmem,
        scratch_shapes=[
            pltpu.VMEM(pixels.shape, pixels.dtype),
            pltpu.VMEM(inv_var.shape, inv_var.dtype),
            pltpu.VMEM(model.shape[1:], model.dtype),
            pltpu.VMEM(row_tr.shape, row_tr.dtype),
            pltpu.VMEM(col_tr.shape, col_tr.dtype),
            dma((5,)),
            pltpu.VMEM((owners, capacity, 2, m, m), jnp.bfloat16),
            pltpu.VMEM((owners, capacity, 2, m, m), jnp.bfloat16),
            pltpu.VMEM((owners, 1, LANES), jnp.int32),
            pltpu.SMEM((1, LANES), jnp.int32),
            pltpu.VMEM((bands, m, side), jnp.float32),
            pltpu.VMEM((bands, m, side), jnp.float32),
            pltpu.VMEM((bands, reach + side, m), jnp.float32),
            pltpu.VMEM((capacity, side, m), jnp.bfloat16),
            pltpu.VMEM((capacity + 1, m, side), jnp.bfloat16),
            pltpu.VMEM((bands, side, side), jnp.float32),
            pltpu.VMEM((groups, bands, rows, side), jnp.bfloat16),
            pltpu.VMEM((groups, bands, rows, side), jnp.bfloat16),
            dma((owners,)),
            dma((owners,)),
            dma((owners,)),
            dma((owners,)),
            dma,
            dma((groups,)),
            dma((groups,)),
        ],
        compiler_params=pltpu.CompilerParams(
            collective_id=0, has_side_effects=True, vmem_limit_bytes=56 * 1024 * 1024
        ),
    )(packed, packed[:, None, :], pixels, inv_var, model[0], row_tr, col_tr)
    return result[None]


def solution(mesh):
    in_specs = (
        P("tile", None, None, None),
        P(("tile", "expo"), None),
        P(("tile", "expo")),
        P(("tile", "expo"), None),
        P(("tile", "expo"), None, None),
        P(("tile", "expo"), None, None),
        P(),
        P(),
    )
    out_specs = P("tile", None, "expo", None)
    return jax.shard_map(local, mesh=mesh, in_specs=in_specs, out_specs=out_specs, check_vma=False)
```

```python
import functools

import jax
import jax.numpy as jnp
from jax import lax
from jax.experimental import pallas as pl
from jax.experimental.pallas import tpu as pltpu
from jax.sharding import PartitionSpec as P

AHEAD = 6
LANES = 128


def slot_layout(exp_tile, exp_band, exp_offset, owners):
    target = exp_tile[:, 0]
    count = target.shape[0]
    order = jnp.arange(count, dtype=jnp.int32)
    before = (target[:, None] == target[None, :]) & (order[None, :] < order[:, None])
    rank = jnp.sum(before.astype(jnp.int32), axis=1)
    packed = 1 + 2 * exp_band + 16 * exp_offset[:, 0] + 2048 * exp_offset[:, 1] + 262144 * order
    owner_hot = target[:, None] == jnp.arange(owners, dtype=jnp.int32)[None, :]
    slot_hot = rank[:, None] == jnp.arange(LANES, dtype=jnp.int32)[None, :]
    hot = owner_hot[:, :, None] & slot_hot[:, None, :]
    return jnp.sum(jnp.where(hot, packed[:, None, None], 0), axis=0)


def partner(me, step, owners):
    if owners == 8:
        third = (step + 1) // 4 - step // 4 - (step + 1) // 8 + step // 8
        fourth = step // 4 - (step + 3) // 8
        step = step + third - fourth
    out = 0
    bit = 1
    while bit < owners:
        out = out + bit * (((me // bit) % 2 + (step // bit) % 2) % 2)
        bit *= 2
    return out


def kernel(
    owners, groups, capacity,
    meta_smem, meta_out, pixels_hbm, inv_var_hbm, model_hbm, row_hbm, col_hbm,
    out,
    pixels, inv_var, model, row_op, col_op, load_sem,
    send, recv, meta_in, meta_s, row_wide, col_wide, row_tall, backs, cols, acc, zsend, zrecv,
    send_sem, recv_sem, msend_sem, mrecv_sem, local_sem, zsend_sem, zrecv_sem,
):
    me = lax.axis_index("tile")
    depth = lax.axis_index("expo")
    bands, side, _ = acc.shape
    q, m = row_op.shape[1:]
    reach = side - q
    rows = side // groups
    together = 3 if capacity % 3 == 0 else (2 if capacity % 2 == 0 else 1)

    loads = [
        pltpu.make_async_copy(source, target, load_sem.at[i])
        for i, (source, target) in enumerate(
            (
                (pixels_hbm, pixels),
                (inv_var_hbm, inv_var),
                (row_hbm, row_op),
                (col_hbm, col_op),
                (model_hbm, model),
            )
        )
    ]
    for load in loads:
        load.start()
    barrier = pltpu.get_barrier_semaphore()

    def greet_tile(j, carry):
        pl.semaphore_signal(
            barrier, inc=1, device_id={"tile": partner(me, j, owners)},
            device_id_type=pl.DeviceIdType.MESH,
        )
        return carry

    def greet_expo(j, carry):
        pl.semaphore_signal(
            barrier, inc=1, device_id={"expo": lax.rem(depth + j, groups)},
            device_id_type=pl.DeviceIdType.MESH,
        )
        return carry

    lax.fori_loop(1, owners, greet_tile, 0)
    lax.fori_loop(1, groups, greet_expo, 0)

    def fill(j, into):
        peer = partner(me, j, owners)

        def one(s, carry):
            e = meta_smem[peer, s] // 262144
            into[j, s, 0] = pixels[e]
            into[j, s, 1] = inv_var[e]
            return carry

        lax.fori_loop(0, capacity, one, 0)

    def data_copy(j):
        return pltpu.make_async_remote_copy(
            send.at[j], recv.at[j], send_sem.at[j], recv_sem.at[j],
            device_id={"tile": partner(me, j, owners)}, device_id_type=pl.DeviceIdType.MESH,
        )

    def meta_copy(j):
        peer = partner(me, j, owners)
        return pltpu.make_async_remote_copy(
            meta_out.at[peer], meta_in.at[j], msend_sem.at[j], mrecv_sem.at[j],
            device_id={"tile": peer}, device_id_type=pl.DeviceIdType.MESH,
        )

    loads[0].wait()
    loads[1].wait()
    fill(1, send)
    pl.semaphore_wait(barrier, owners + groups - 2)

    def push_meta(j, carry):
        meta_copy(j).start()
        return carry

    lax.fori_loop(1, owners, push_meta, 0)

    def push(j, carry):
        @pl.when(j > 1)
        def _():
            fill(j, send)

        data_copy(j).start()
        return carry

    ahead = min(AHEAD, owners - 1)
    lax.fori_loop(1, ahead + 1, push, 0)

    fill(0, recv)
    acc[...] = jnp.zeros_like(acc)
    cols[capacity] = jnp.zeros_like(cols[capacity])

    for load in loads[2:]:
        load.wait()

    def widen(b, carry):
        zeros = jnp.zeros((reach, m), jnp.float32)
        r = jnp.concatenate([row_op[b].astype(jnp.float32), zeros], axis=0)
        c = jnp.concatenate([col_op[b].astype(jnp.float32), zeros], axis=0)
        row_wide[b] = r.T
        col_wide[b] = c.T
        row_tall[b, 0:reach, :] = zeros
        row_tall[b, reach : reach + side, :] = r
        return carry

    lax.fori_loop(0, bands, widen, 0)

    def block(z):
        return pl.ds(pl.multiple_of(z * rows, rows), rows)

    def z_copy(j, b):
        return pltpu.make_async_remote_copy(
            zsend.at[j, b], zrecv.at[j, b], zsend_sem.at[j, b], zrecv_sem.at[j, b],
            device_id={"expo": lax.rem(depth + j, groups)}, device_id_type=pl.DeviceIdType.MESH,
        )

    def z_push(b):
        def one(j, carry):
            zsend[j, b] = acc[b, block(lax.rem(depth + j, groups)), :].astype(jnp.bfloat16)
            z_copy(j, b).start()
            return carry

        lax.fori_loop(1, groups, one, 0)

    def compute(j):
        def some_slots(t, carry):
            slots = [t * together + u for u in range(together)]
            wide, cut = [], []
            for s in slots:
                code = meta_s[j, 0, s]
                band, row, col = code // 2 % 8, code // 16 % 128, code // 2048 % 128
                r = pltpu.roll(row_wide[band], row, 1).astype(jnp.bfloat16)
                c = pltpu.roll(col_wide[band], col, 1).astype(jnp.bfloat16)
                rt = row_tall[band, pl.ds(reach - row, side), :].astype(jnp.bfloat16)
                cols[s] = c
                wide.append((r, c, rt, band))
            halfs = [
                jnp.dot(r, model[band], preferred_element_type=jnp.float32).astype(jnp.bfloat16)
                for r, c, rt, band in wide
            ]
            predicted = [
                lax.dot_general(
                    h, w[1], (((1,), (1,)), ((), ())), preferred_element_type=jnp.float32
                )
                for h, w in zip(halfs, wide)
            ]
            weighted = [
                (
                    recv[j, s, 1].astype(jnp.float32) * (p - recv[j, s, 0].astype(jnp.float32))
                ).astype(jnp.bfloat16)
                for p, s in zip(predicted, slots)
            ]
            for w, x, s in zip(wide, weighted, slots):
                backs[s] = jnp.dot(w[2], x, preferred_element_type=jnp.float32).astype(
                    jnp.bfloat16
                )
            return carry

        lax.fori_loop(0, capacity // together, some_slots, 0)

        def one_band(b, carry):
            left = jnp.concatenate([backs[s] for s in range(capacity)], axis=1)
            right = []
            for s in range(capacity):
                mine = meta_s[j, 0, s] % 16 == 2 * b + 1
                right.append(cols[jnp.where(mine, s, capacity)])
            acc[b] += jnp.dot(
                left, jnp.concatenate(right, axis=0), preferred_element_type=jnp.float32
            )

            @pl.when(j == owners - 1)
            def _():
                z_push(b)

            return carry

        lax.fori_loop(0, bands, one_band, 0)

    def fetch_meta(j, source):
        copy = pltpu.make_async_copy(source, meta_s.at[j], local_sem)
        copy.start()
        copy.wait()

    fetch_meta(0, meta_out.at[me])
    compute(jnp.int32(0))

    def arrive(j, carry):
        meta_copy(j).wait_recv()
        fetch_meta(j, meta_in.at[j])
        return carry

    lax.fori_loop(1, owners, arrive, 0)

    def turn(j, carry):
        data_copy(j).wait_recv()

        @pl.when(j + ahead < owners)
        def _():
            push(j + ahead, 0)

        compute(j)
        return carry

    lax.fori_loop(1, owners, turn, 0)

    out[...] = acc[:, block(depth), :]

    def z_sum(j, carry):
        b, peer = j // (groups - 1), j % (groups - 1) + 1
        z_copy(peer, b).wait_recv()
        out[b] += zrecv[peer, b].astype(jnp.float32)
        return carry

    lax.fori_loop(0, bands * (groups - 1), z_sum, 0)

    def finish(j, carry):
        meta_copy(j).wait_send()
        data_copy(j).wait_send()
        return carry

    lax.fori_loop(1, owners, finish, 0)

    def z_finish(j, carry):
        z_copy(j % (groups - 1) + 1, j // (groups - 1)).wait_send()
        return carry

    lax.fori_loop(0, bands * (groups - 1), z_finish, 0)


def local(model, exp_tile, exp_band, exp_offset, pixels, inv_var, row_op, col_op):
    owners = lax.axis_size("tile")
    groups = lax.axis_size("expo")
    count, m, _ = pixels.shape
    capacity = max(2, 3 * count // (2 * owners))
    bands, side = model.shape[1], model.shape[2]
    q = row_op.shape[2]
    reach = side - q
    rows = side // groups
    packed = slot_layout(exp_tile, exp_band, exp_offset, owners)
    row_tr, col_tr = jnp.swapaxes(row_op, 1, 2), jnp.swapaxes(col_op, 1, 2)
    hbm = pl.BlockSpec(memory_space=pl.ANY)
    vmem = pl.BlockSpec(memory_space=pltpu.VMEM)
    dma = pltpu.SemaphoreType.DMA
    result = pl.pallas_call(
        functools.partial(kernel, owners, groups, capacity),
        out_shape=jax.ShapeDtypeStruct((bands, rows, side), jnp.float32),
        in_specs=[pl.BlockSpec(memory_space=pltpu.SMEM), vmem] + [hbm] * 5,
        out_specs=vmem,
        scratch_shapes=[
            pltpu.VMEM(pixels.shape, pixels.dtype),
            pltpu.VMEM(inv_var.shape, inv_var.dtype),
            pltpu.VMEM(model.shape[1:], model.dtype),
            pltpu.VMEM(row_tr.shape, row_tr.dtype),
            pltpu.VMEM(col_tr.shape, col_tr.dtype),
            dma((5,)),
            pltpu.VMEM((owners, capacity, 2, m, m), jnp.bfloat16),
            pltpu.VMEM((owners, capacity, 2, m, m), jnp.bfloat16),
            pltpu.VMEM((owners, 1, LANES), jnp.int32),
            pltpu.SMEM((owners, 1, LANES), jnp.int32),
            pltpu.VMEM((bands, m, side), jnp.float32),
            pltpu.VMEM((bands, m, side), jnp.float32),
            pltpu.VMEM((bands, reach + side, m), jnp.float32),
            pltpu.VMEM((capacity, side, m), jnp.bfloat16),
            pltpu.VMEM((capacity + 1, m, side), jnp.bfloat16),
            pltpu.VMEM((bands, side, side), jnp.float32),
            pltpu.VMEM((groups, bands, rows, side), jnp.bfloat16),
            pltpu.VMEM((groups, bands, rows, side), jnp.bfloat16),
            dma((owners,)),
            dma((owners,)),
            dma((owners,)),
            dma((owners,)),
            dma,
            dma((groups, bands)),
            dma((groups, bands)),
        ],
        compiler_params=pltpu.CompilerParams(
            collective_id=0, has_side_effects=True, vmem_limit_bytes=56 * 1024 * 1024
        ),
    )(packed, packed[:, None, :], pixels, inv_var, model[0], row_tr, col_tr)
    return result[None]


def solution(mesh):
    in_specs = (
        P("tile", None, None, None),
        P(("tile", "expo"), None),
        P(("tile", "expo")),
        P(("tile", "expo"), None),
        P(("tile", "expo"), None, None),
        P(("tile", "expo"), None, None),
        P(),
        P(),
    )
    out_specs = P("tile", None, "expo", None)
    return jax.shard_map(local, mesh=mesh, in_specs=in_specs, out_specs=out_specs, check_vma=False)
```
